1024 devices in a mesh: span: 16 (over y, core), head: 16 (over z), rep: 4 (over x).
Axes of the slice: x: 4, y: 8, z: 16, core: 2. Of those that a mesh axis runs over, the one named last changes fastest.
Arguments:
- queries: bfloat16 [131072, 4096], P(('rep', 'span', 'head')), parts along dimension 0, may hold values from -9 to 9
- keys: bfloat16 [131072, 512], P(('rep', 'span', 'head')), parts along dimension 0, may hold values from -9 to 9
- values: bfloat16 [131072, 512], P(('rep', 'span', 'head')), parts along dimension 0, may hold values from -6 to 6
- out_grad: bfloat16 [131072, 4096], P(('rep', 'span'), 'head'), parts along dimension 0, may hold values from -6 to 6
- doc_lengths: int32 [128], P('rep'), parts along dimension 0, may hold values from 1 to 4096, 32768 in all
Outputs:
- key_value_grads: bfloat16 [1024, 131072], P('head', ('rep', 'span')), parts along dimension 1
- log_totals: float32 [32, 131072], P('head', ('rep', 'span')), parts along dimension 1
The draws below stay inside these ranges and needn't reach their ends.
There are 4 independent parts, one for each index of `rep`. The reference program is written for one: setup_inputs(seed, part) draws one part's arguments, and reference() takes and returns one part's arrays. A program takes and returns all parts, laid end to end along the dimension named above; each array names one. Nothing has to cross between parts.
Inputs may be any that keep to these rules, and one draw needn't show every extreme that they name: `doc_lengths`: they sum to 32768; the longest is exactly 4096.
All inputs are finite; a program needn't handle non-finite values.
Results may differ from the reference program's by a relative error of at most 0.0068.
Values may be sent and summed in bfloat16 or wider, within the bound.
No kernel may reach another device: no remote copies, remote signals or barrier semaphores. Data moves between devices by JAX's collectives and lax.ppermute only.
A program may use at most 32 MiB of HBM per device.

```python
import math
import jax
import jax.numpy as jnp
import numpy as np
from jax import lax

HEADS = 32
KV_HEADS = 4
HEAD_DIM = 128
BLOCK = 128
WINDOW = 2
TOKENS = 32768
HALO = 128
MOST_DOC = 4096
DOCS = 32


def draw_queries(key, part):
    fresh_key = jax.random.fold_in(key, 11)
    drawn = jax.random.truncated_normal(fresh_key, -6.0, 6.0, (TOKENS, HEADS * HEAD_DIM), jnp.float32)
    return drawn.astype(jnp.bfloat16)


def draw_keys(key, part):
    fresh_key = jax.random.fold_in(key, 13)
    drawn = jax.random.truncated_normal(fresh_key, -6.0, 6.0, (TOKENS, KV_HEADS * HEAD_DIM), jnp.float32)
    return drawn.astype(jnp.bfloat16)


def block_levels(rng, extent, pieces, least, high):
    loudness, own = 1.0, jax.random.fold_in(rng, 6)
    for position, parts in pieces:
        steps = jnp.exp(jax.random.uniform(jax.random.fold_in(own, position), (parts,), jnp.float32, least / len(pieces), high / len(pieces)))
        loudness = loudness * jnp.repeat(steps, extent[position] // parts).reshape([-1 if axis == position else 1 for axis in range(len(extent))])
    return loudness


def profile(number_of, total, most, lean):
    weights = [(1 << 20) // math.isqrt(rank ** lean) + 1 for rank in range(2, number_of + 1)]
    rest, holding = total - most - (number_of - 1), [1] * (number_of - 1)
    while rest > 0:
        movable = [i for i in range(number_of - 1) if holding[i] < most]
        pool, remaining = sum([weights[i] for i in movable]), rest
        for i in movable:
            more = min(most - holding[i], max(1, remaining * weights[i] // pool), rest)
            holding[i] = holding[i] + more
            rest = rest - more
    return np.array([most] + holding)


def ragged_sizes(own_key, number_of, total, bound, lean):
    if number_of == 2:
        one = jax.random.randint(own_key, (), max(1, total - bound), min(bound, total - 1) + 1)
        return jnp.stack([one, total - one])
    lengths = jnp.asarray(profile(number_of, total, bound, lean), jnp.int32)
    couples = (number_of - 1) // 2
    source_of, sink = lengths[1:1 + 2 * couples:2], lengths[2:2 + 2 * couples:2]
    margin = jnp.minimum(source_of - 1, bound - sink)
    moved = jax.random.randint(jax.random.fold_in(own_key, 1), (couples,), 0, 1 << 20) % (margin + 1)
    lengths = lengths.at[1:1 + 2 * couples:2].set(source_of - moved).at[2:2 + 2 * couples:2].set(sink + moved)
    return lengths[jax.random.permutation(jax.random.fold_in(own_key, 2), number_of)]


def gaussian(own_key, extent, scale, most, cuts=(), kind=jnp.bfloat16):
    entries = jax.random.normal(own_key, extent, jnp.float32) * scale
    if len(cuts) > 0:
        entries = block_levels(own_key, extent, cuts, -0.22, 0.18) * entries
    return jnp.clip(entries, min=-most, max=most).astype(kind)


def setup_inputs(seed: int = 0, part: int = 0) -> dict:
    arg_keys = jax.random.split(jax.random.key(seed), 6)
    part_splits = jax.random.split(jax.random.fold_in(arg_keys[5], part), 6)
    queries = draw_queries(jax.random.fold_in(jax.random.fold_in(arg_keys[5], part), 71), part)
    keys = draw_keys(jax.random.fold_in(jax.random.fold_in(arg_keys[5], part), 71), part)
    values = gaussian(part_splits[2], (TOKENS, KV_HEADS * HEAD_DIM), 1.0, 6.0, ((0, 256),))
    out_grad = gaussian(part_splits[3], (TOKENS, HEADS * HEAD_DIM), 1.0, 6.0, ((0, 16), (1, 16)))
    doc_lengths = ragged_sizes(part_splits[4], DOCS, TOKENS, MOST_DOC, 2).astype(jnp.int32)
    return dict(queries=queries, keys=keys, values=values, out_grad=out_grad, doc_lengths=doc_lengths)


def document_starts(doc_lengths, positions):
    doc_starts = (jnp.cumsum(doc_lengths) - doc_lengths).astype(jnp.int32)
    inside = doc_starts[None, :] <= positions[:, None]
    return lax.optimization_barrier(jnp.max(jnp.where(inside, doc_starts[None, :], 0), axis=1)).astype(jnp.int32)

def reference(queries, keys, values, out_grad, doc_lengths):
    score_scale = 1.0 / math.sqrt(HEAD_DIM)
    group_size = HEADS // KV_HEADS
    width = WINDOW * BLOCK
    n_blocks = TOKENS // BLOCK
    query_heads = queries.reshape(TOKENS, KV_HEADS, group_size, HEAD_DIM)
    grad_heads = out_grad.reshape(TOKENS, KV_HEADS, group_size, HEAD_DIM)
    padding = jnp.zeros((HALO, KV_HEADS, HEAD_DIM), jnp.bfloat16)
    key_pad = jnp.concatenate([padding, keys.reshape(TOKENS, KV_HEADS, HEAD_DIM)], 0)
    value_pad = jnp.concatenate([padding, values.reshape(TOKENS, KV_HEADS, HEAD_DIM)], 0)
    block_offsets = jnp.arange(BLOCK, dtype=jnp.int32)
    window_offsets = jnp.arange(width, dtype=jnp.int32)

    def block_step(carry, block_index):
        key_grad, value_grad = carry
        first_row = block_index * BLOCK
        query_block = lax.dynamic_slice_in_dim(query_heads, first_row, BLOCK, 0).astype(jnp.float32)
        grad_block = lax.dynamic_slice_in_dim(grad_heads, first_row, BLOCK, 0).astype(jnp.float32)
        key_window = lax.dynamic_slice_in_dim(key_pad, first_row, width, 0).astype(jnp.float32)
        value_window = lax.dynamic_slice_in_dim(value_pad, first_row, width, 0).astype(jnp.float32)
        query_pos = first_row + block_offsets
        key_pos = first_row - HALO + window_offsets
        doc_first = document_starts(doc_lengths, query_pos)
        allowed = (key_pos[None, :] >= doc_first[:, None]) & (key_pos[None, :] <= query_pos[:, None])
        scores = jnp.einsum('qkgd,jkd->kgqj', query_block, key_window) * score_scale
        scores = jnp.where(allowed[None, None], scores, -1e+30)
        row_max = lax.optimization_barrier(jnp.max(scores, axis=-1, keepdims=True))
        exponent = jnp.exp(scores - row_max)
        row_total = lax.optimization_barrier(jnp.sum(exponent, axis=-1, keepdims=True))
        weights = exponent / row_total
        log_totals = (row_max + jnp.log(row_total))[..., 0]
        weights_low = lax.optimization_barrier(weights.astype(jnp.bfloat16)).astype(jnp.float32)
        attention = jnp.einsum('kgqj,jkd->qkgd', weights_low, value_window).astype(jnp.bfloat16)
        attention = lax.optimization_barrier(attention).astype(jnp.float32)
        dweights = jnp.einsum('qkgd,jkd->kgqj', grad_block, value_window)
        delta_rows = jnp.einsum('qkgd,qkgd->kgq', grad_block, attention)
        dscores = (weights * (dweights - delta_rows[..., None])).astype(jnp.bfloat16)
        dscores = lax.optimization_barrier(dscores).astype(jnp.float32)
        key_part = jnp.einsum('kgqj,qkgd->jkd', dscores, query_block) * score_scale
        value_part = jnp.einsum('kgqj,qkgd->jkd', weights_low, grad_block)
        key_grad = lax.dynamic_update_slice_in_dim(key_grad, lax.dynamic_slice_in_dim(key_grad, first_row, width, 0) + key_part, first_row, 0)
        value_grad = lax.dynamic_update_slice_in_dim(value_grad, lax.dynamic_slice_in_dim(value_grad, first_row, width, 0) + value_part, first_row, 0)
        return ((key_grad, value_grad), log_totals.reshape(HEADS, BLOCK))
    zeros_init = jnp.zeros((TOKENS + HALO, KV_HEADS, HEAD_DIM), jnp.float32)
    (key_grad, value_grad), total_blocks = lax.scan(block_step, (zeros_init, zeros_init), jnp.arange(n_blocks, dtype=jnp.int32))
    log_totals = jnp.transpose(total_blocks, (1, 0, 2)).reshape(HEADS, TOKENS)
    stacked = jnp.stack([key_grad[HALO:], value_grad[HALO:]], axis=2)
    key_value_grads = jnp.transpose(stacked, (1, 2, 3, 0)).reshape(2 * KV_HEADS * HEAD_DIM, TOKENS)
    return (key_value_grads.astype(jnp.bfloat16), log_totals)
```

```python
import math

import jax
import jax.numpy as jnp
from jax import lax
from jax.experimental import pallas as pl
from jax.experimental.pallas import tpu as pltpu
from jax.sharding import PartitionSpec as P

HEADS = 32
KV_HEADS = 4
GROUP = HEADS // KV_HEADS
HEAD_DIM = 128
BLOCK = 128
WIDTH = 2 * BLOCK
DOCS = 32
OWNERS = 16
OWNED = 2 * KV_HEADS * HEAD_DIM // OWNERS
HEADS_OWNED = HEADS // OWNERS
EXTRA = 8
SCALE = 1.0 / math.sqrt(HEAD_DIM)
NEG = -1e30
VMEM = pl.BlockSpec(memory_space=pltpu.VMEM)
SMEM = pl.BlockSpec(memory_space=pltpu.SMEM)
NT = (((1,), (1,)), ((), ()))


def dot(a, b, dims=(((1,), (0,)), ((), ()))):
    return lax.dot_general(a, b, dims, preferred_element_type=jnp.float32)


def head_cols(h):
    return slice(h * HEAD_DIM, (h + 1) * HEAD_DIM)


def forward_kernel(base_ref, doc_ref, q_ref, k_ref, k_prev_ref, p_ref, total_ref):
    base = base_ref[0]
    query_pos = base + lax.broadcasted_iota(jnp.int32, (1, BLOCK), 1)
    doc_first = jnp.zeros((1, BLOCK), jnp.int32)
    start = jnp.int32(0)
    for d in range(DOCS):
        doc_first = jnp.where(start <= query_pos, start, doc_first)
        start = start + doc_ref[d]
    key_pos = base - BLOCK + lax.broadcasted_iota(jnp.int32, (WIDTH, BLOCK), 0)
    allowed = (key_pos >= doc_first) & (key_pos <= query_pos)
    bias = jnp.where(allowed, 0.0, NEG)
    for g in range(KV_HEADS):
        keys = jnp.concatenate([k_prev_ref[:, head_cols(g)], k_ref[:, head_cols(g)]], 0)
        for h in range(GROUP):
            head = g * GROUP + h
            s = dot(keys, q_ref[:, head_cols(head)], NT) * (SCALE * math.log2(math.e)) + bias
            row_max = jnp.max(s, axis=0, keepdims=True)
            e = jnp.exp2(s - row_max)
            total = jnp.sum(e, axis=0, keepdims=True)
            p_ref[g, :, head_cols(h)] = (e * (1.0 / total)).astype(jnp.bfloat16)
            total_ref[head : head + 1, :] = (row_max + jnp.log2(total)) * math.log(2.0)


def backward_kernel(p_ref, og_ref, q_ref, v_ref, v_prev_ref, own_ref, halo_ref, ds_ref):
    for g in range(KV_HEADS):
        vals = jnp.concatenate([v_prev_ref[:, head_cols(g)], v_ref[:, head_cols(g)]], 0)
        grads = []
        for h in range(GROUP):
            head = g * GROUP + h
            og = og_ref[head // HEADS_OWNED, :, head_cols(head % HEADS_OWNED)]
            grads.append(og)
            dp = dot(vals, og, NT)
            p = p_ref[g, :, head_cols(h)].astype(jnp.float32)
            delta = jnp.sum(p * dp, axis=0, keepdims=True)
            ds_ref[:, head_cols(h)] = (p * (dp - delta)).astype(jnp.bfloat16)
        queries = jnp.concatenate(
            [q_ref[:, head_cols(g * GROUP + h)] for h in range(GROUP)], 0
        )
        dk = (dot(ds_ref[...], queries) * SCALE).T
        dv = dot(p_ref[g], jnp.concatenate(grads, 0)).T
        for i, grad in enumerate((dk, dv)):
            rows = slice((2 * g + i) * HEAD_DIM, (2 * g + i + 1) * HEAD_DIM)
            halo_ref[rows, :] = grad[:, :BLOCK].astype(jnp.bfloat16)
            own_ref[rows, :] = grad[:, BLOCK:]


def sum_kernel(own_ref, halo_ref, total_ref, send_ref):
    for z in range(OWNERS):
        rows = slice(z * OWNED, (z + 1) * OWNED)
        send_ref[z, :OWNED, :] = (
            own_ref[rows, :] + halo_ref[rows, :].astype(jnp.float32)
        ).astype(jnp.bfloat16)
        total = total_ref[z * HEADS_OWNED : (z + 1) * HEADS_OWNED, :]
        high = total.astype(jnp.bfloat16).astype(jnp.float32)
        low = total - high
        pad = jnp.zeros((EXTRA - 2 * HEADS_OWNED, BLOCK), jnp.float32)
        send_ref[z, OWNED:, :] = jnp.concatenate([high, low, pad], 0).astype(jnp.bfloat16)


def unpack_kernel(got_ref, grads_ref, total_ref):
    for b in range(OWNERS):
        cols = slice(b * BLOCK, (b + 1) * BLOCK)
        grads_ref[:, cols] = got_ref[b, :OWNED, :]
        extra = got_ref[b, OWNED:, :].astype(jnp.float32)
        total_ref[:, cols] = extra[:HEADS_OWNED] + extra[HEADS_OWNED : 2 * HEADS_OWNED]


def call(kernel, out_shape, args, specs, scratch=(), flops=0, exps=0):
    outs = jax.tree.leaves(out_shape)
    moved = sum(math.prod(a.shape) * a.dtype.itemsize for a in [*args, *outs])
    return pl.pallas_call(
        kernel,
        out_shape=out_shape,
        in_specs=specs,
        out_specs=jax.tree.map(lambda _: VMEM, out_shape),
        scratch_shapes=scratch,
        compiler_params=pltpu.CompilerParams(vmem_limit_bytes=40 * 2**20),
        cost_estimate=pl.CostEstimate(
            flops=flops, bytes_accessed=moved, transcendentals=exps
        ),
    )(*args)


def shards(queries, keys, values, out_grad, doc_lengths):
    spans, owners = lax.axis_size("span"), lax.axis_size("head")
    block_index = lax.axis_index("span") * owners + lax.axis_index("head")
    blocks = spans * owners
    base = jnp.full((1,), block_index * BLOCK, jnp.int32)
    f32, bf16 = jnp.float32, jnp.bfloat16
    onward = [(i, i + 1) for i in range(blocks - 1)]
    back = [(i + 1, i) for i in range(blocks - 1)]
    og = lax.all_to_all(
        out_grad.reshape(owners, BLOCK, HEADS_OWNED * HEAD_DIM), "head", 0, 0, tiled=True
    )
    k_prev = lax.ppermute(keys, ("span", "head"), onward)
    v_prev = lax.ppermute(values, ("span", "head"), onward)
    macs = HEADS * BLOCK * WIDTH * HEAD_DIM
    weights, totals = call(
        forward_kernel,
        (
            jax.ShapeDtypeStruct((KV_HEADS, WIDTH, GROUP * BLOCK), bf16),
            jax.ShapeDtypeStruct((HEADS, BLOCK), f32),
        ),
        (base, doc_lengths, queries, keys, k_prev),
        [SMEM, SMEM, VMEM, VMEM, VMEM],
        flops=2 * macs,
        exps=HEADS * BLOCK * WIDTH,
    )
    features = 2 * KV_HEADS * HEAD_DIM
    own, halo = call(
        backward_kernel,
        (
            jax.ShapeDtypeStruct((features, BLOCK), f32),
            jax.ShapeDtypeStruct((features, BLOCK), bf16),
        ),
        (weights, og, queries, values, v_prev),
        [VMEM] * 5,
        scratch=[pltpu.VMEM((WIDTH, GROUP * BLOCK), bf16)],
        flops=6 * macs,
    )
    returned = lax.ppermute(halo, ("span", "head"), back)
    send = call(
        sum_kernel,
        jax.ShapeDtypeStruct((owners, OWNED + EXTRA, BLOCK), bf16),
        (own, returned, totals),
        [VMEM] * 3,
    )
    got = lax.all_to_all(send, "head", 0, 0, tiled=True)
    return call(
        unpack_kernel,
        (
            jax.ShapeDtypeStruct((OWNED, owners * BLOCK), bf16),
            jax.ShapeDtypeStruct((HEADS_OWNED, owners * BLOCK), f32),
        ),
        (got,),
        [VMEM],
    )


def solution(mesh):
    return jax.shard_map(
        shards,
        mesh=mesh,
        in_specs=(
            P(("rep", "span", "head"), None),
            P(("rep", "span", "head"), None),
            P(("rep", "span", "head"), None),
            P(("rep", "span"), "head"),
            P("rep"),
        ),
        out_specs=(P("head", ("rep", "span")), P("head", ("rep", "span"))),
        check_vma=False,
    )
```

```python
import math

import jax
import jax.numpy as jnp
from jax import lax
from jax.experimental import pallas as pl
from jax.experimental.pallas import tpu as pltpu
from jax.sharding import PartitionSpec as P

HEADS = 32
KV_HEADS = 4
GROUP = HEADS // KV_HEADS
HEAD_DIM = 128
BLOCK = 128
WIDTH = 2 * BLOCK
DOCS = 32
OWNERS = 16
OWNED = 2 * KV_HEADS * HEAD_DIM // OWNERS
HEADS_OWNED = HEADS // OWNERS
EXTRA = 8
SCALE = 1.0 / math.sqrt(HEAD_DIM)
SCORE_SCALE = SCALE * math.log2(math.e)
NEG = -1e30
PAIRS = GROUP // 2
VMEM = pl.BlockSpec(memory_space=pltpu.VMEM)
SMEM = pl.BlockSpec(memory_space=pltpu.SMEM)
NT = (((1,), (1,)), ((), ()))


def dot(a, b, dims=(((1,), (0,)), ((), ()))):
    return lax.dot_general(a, b, dims, preferred_element_type=jnp.float32)


def pair_rows(ref, pair):
    left = 2 * pair * HEAD_DIM
    return jnp.concatenate(
        [ref[:, left : left + HEAD_DIM], ref[:, left + HEAD_DIM : left + 2 * HEAD_DIM]], 0
    )


def pair_cols(pair):
    return slice(2 * pair * BLOCK, 2 * (pair + 1) * BLOCK)


def twice(x):
    return jnp.concatenate([x, x], 1)


def feature_rows(group, which):
    first = (2 * group + which) * HEAD_DIM
    return slice(first, first + HEAD_DIM)


def head_cols(h):
    return slice(h * HEAD_DIM, (h + 1) * HEAD_DIM)


def own_scores_kernel(
    base_ref, doc_ref, q_ref, k_ref, v_ref, e_ref, stats_ref, bias_ref, q_out_ref, v_out_ref
):
    q_out_ref[...] = q_ref[...]
    v_out_ref[...] = v_ref[...]
    base = base_ref[0]
    query_pos = base + lax.broadcasted_iota(jnp.int32, (1, BLOCK), 1)
    doc_first = jnp.zeros((1, BLOCK), jnp.int32)
    start = jnp.int32(0)
    for d in range(DOCS):
        doc_first = jnp.where(start <= query_pos, start, doc_first)
        start = start + doc_ref[d]
    key_pos = base + lax.broadcasted_iota(jnp.int32, (BLOCK, BLOCK), 0)
    bias_ref[...] = jnp.where(key_pos - BLOCK >= doc_first, 0.0, NEG)
    bias = twice(jnp.where((key_pos >= doc_first) & (key_pos <= query_pos), 0.0, NEG))
    for g in range(KV_HEADS):
        for i in range(PAIRS):
            pair = g * PAIRS + i
            s = dot(k_ref[:, head_cols(g)], pair_rows(q_ref, pair), NT) * SCORE_SCALE + bias
            row_max = jnp.max(s, axis=0, keepdims=True)
            e = jnp.exp2(s - row_max)
            e_ref[g, :, pair_cols(i)] = e
            stats_ref[0, pair : pair + 1, :] = row_max
            stats_ref[1, pair : pair + 1, :] = jnp.sum(e, axis=0, keepdims=True)


def halo_kernel(
    e_ref, stats_ref, bias_ref, q_ref, v_ref, k_far_ref, v_far_ref, og_far_ref,
    halo_ref, p_ref, ds_ref, total_ref, og_ref, p_prev_ref, ds_prev_ref, k_prev_ref, v_prev_ref, sems,
):
    copies = [
        pltpu.make_async_copy(k_far_ref, k_prev_ref, sems.at[KV_HEADS]),
        pltpu.make_async_copy(v_far_ref, v_prev_ref, sems.at[KV_HEADS + 1]),
    ]
    og_copies = [
        pltpu.make_async_copy(
            og_far_ref.at[pl.ds(g * PAIRS, PAIRS)], og_ref.at[pl.ds(g * PAIRS, PAIRS)], sems.at[g]
        )
        for g in range(KV_HEADS)
    ]
    for copy in copies + og_copies:
        copy.start()
    for copy in copies:
        copy.wait()
    bias = twice(bias_ref[...])
    for g in range(KV_HEADS):
        og_copies[g].wait()
        vals = jnp.concatenate([v_prev_ref[:, head_cols(g)], v_ref[:, head_cols(g)]], 0)
        queries, grads = [], []
        for i in range(PAIRS):
            pair = g * PAIRS + i
            q = pair_rows(q_ref, pair)
            og = pair_rows(og_ref.at[pair], 0)
            queries.append(q)
            grads.append(og)
            s = dot(k_prev_ref[:, head_cols(g)], q, NT) * SCORE_SCALE + bias
            own_max = stats_ref[0, pair : pair + 1, :]
            row_max = jnp.maximum(jnp.max(s, axis=0, keepdims=True), own_max)
            e = jnp.exp2(s - row_max)
            shrink = jnp.exp2(own_max - row_max)
            total = jnp.sum(e, axis=0, keepdims=True) + shrink * stats_ref[1, pair : pair + 1, :]
            total_ref[pair : pair + 1, :] = (row_max + jnp.log2(total)) * math.log(2.0)
            inverse = 1.0 / total
            p_prev = e * inverse
            p_own = e_ref[g, :, pair_cols(i)] * (shrink * inverse)
            dp = dot(vals, og, NT)
            dp_prev, dp_own = dp[:BLOCK], dp[BLOCK:]
            delta = jnp.sum(p_prev * dp_prev, axis=0, keepdims=True) + jnp.sum(
                p_own * dp_own, axis=0, keepdims=True
            )
            p_prev_ref[:, pair_cols(i)] = p_prev.astype(jnp.bfloat16)
            ds_prev_ref[:, pair_cols(i)] = (p_prev * (dp_prev - delta)).astype(jnp.bfloat16)
            p_ref[g, :, pair_cols(i)] = p_own.astype(jnp.bfloat16)
            ds_ref[g, :, pair_cols(i)] = (p_own * (dp_own - delta)).astype(jnp.bfloat16)
        dk = dot(ds_prev_ref[...], jnp.concatenate(queries, 0)) * SCALE
        dv = dot(p_prev_ref[...], jnp.concatenate(grads, 0))
        halo_ref[feature_rows(g, 0), :] = dk.T.astype(jnp.bfloat16)
        halo_ref[feature_rows(g, 1), :] = dv.T.astype(jnp.bfloat16)


def own_kernel(p_ref, ds_ref, q_ref, og_ref, own_ref):
    for g in range(KV_HEADS):
        pairs = range(g * PAIRS, (g + 1) * PAIRS)
        queries = jnp.concatenate([pair_rows(q_ref, pair) for pair in pairs], 0)
        grads = jnp.concatenate([pair_rows(og_ref.at[pair], 0) for pair in pairs], 0)
        own_ref[feature_rows(g, 0), :] = (dot(ds_ref[g], queries) * SCALE).T
        own_ref[feature_rows(g, 1), :] = dot(p_ref[g], grads).T


def sum_kernel(own_ref, halo_ref, total_ref, send_ref):
    for z in range(OWNERS):
        rows = slice(z * OWNED, (z + 1) * OWNED)
        send_ref[z, :OWNED, :] = (
            own_ref[rows, :] + halo_ref[rows, :].astype(jnp.float32)
        ).astype(jnp.bfloat16)
        total = total_ref[z : z + 1, :]
        total = jnp.concatenate([total[:, :BLOCK], total[:, BLOCK:]], 0)
        high = total.astype(jnp.bfloat16).astype(jnp.float32)
        low = total - high
        pad = jnp.zeros((EXTRA - 2 * HEADS_OWNED, BLOCK), jnp.float32)
        send_ref[z, OWNED:, :] = jnp.concatenate([high, low, pad], 0).astype(jnp.bfloat16)


def unpack_kernel(got_ref, grads_ref, total_ref):
    for b in range(OWNERS):
        cols = slice(b * BLOCK, (b + 1) * BLOCK)
        grads_ref[:, cols] = got_ref[b, :OWNED, :]
        extra = got_ref[b, OWNED:, :].astype(jnp.float32)
        total_ref[:, cols] = extra[:HEADS_OWNED] + extra[HEADS_OWNED : 2 * HEADS_OWNED]


def call(kernel, out_shape, args, specs, scratch=(), flops=0, exps=0, limit=8):
    outs = jax.tree.leaves(out_shape)
    moved = sum(math.prod(a.shape) * a.dtype.itemsize for a in [*args, *outs])
    return pl.pallas_call(
        kernel,
        out_shape=out_shape,
        in_specs=specs,
        out_specs=jax.tree.map(lambda _: VMEM, out_shape),
        scratch_shapes=scratch,
        compiler_params=pltpu.CompilerParams(vmem_limit_bytes=limit * 2**20),
        cost_estimate=pl.CostEstimate(
            flops=flops, bytes_accessed=moved, transcendentals=exps
        ),
    )(*args)


def shards(queries, keys, values, out_grad, doc_lengths):
    spans, owners = lax.axis_size("span"), lax.axis_size("head")
    block_index = lax.axis_index("span") * owners + lax.axis_index("head")
    blocks = spans * owners
    base = jnp.full((1,), block_index * BLOCK, jnp.int32)
    f32, bf16 = jnp.float32, jnp.bfloat16
    onward = [(i, i + 1) for i in range(blocks - 1)]
    back = [(i + 1, i) for i in range(blocks - 1)]
    og = lax.all_to_all(
        out_grad.reshape(owners, BLOCK, HEADS_OWNED * HEAD_DIM), "head", 0, 0, tiled=True
    )
    k_prev = lax.ppermute(keys, ("span", "head"), onward)
    v_prev = lax.ppermute(values, ("span", "head"), onward)
    macs = HEADS * BLOCK * BLOCK * HEAD_DIM
    array = jax.ShapeDtypeStruct
    exponents, stats, bias, held_queries, held_values = call(
        own_scores_kernel,
        (
            array((KV_HEADS, BLOCK, GROUP * BLOCK), f32),
            array((2, owners, HEADS_OWNED * BLOCK), f32),
            array((BLOCK, BLOCK), f32),
            array(queries.shape, bf16),
            array(values.shape, bf16),
        ),
        (base, doc_lengths, queries, keys, values),
        [SMEM, SMEM] + [VMEM] * 3,
        flops=20000 * macs,
        exps=HEADS * BLOCK * BLOCK,
    )
    features = 2 * KV_HEADS * HEAD_DIM
    kept = array((KV_HEADS, BLOCK, GROUP * BLOCK), bf16)
    halo, weights, dscores, totals, held_grads = call(
        halo_kernel,
        (
            array((features, BLOCK), bf16),
            kept,
            kept,
            array((owners, HEADS_OWNED * BLOCK), f32),
            array(og.shape, bf16),
        ),
        (exponents, stats, bias, held_queries, held_values, k_prev, v_prev, og),
        [VMEM] * 5 + [pl.BlockSpec(memory_space=pl.ANY)] * 3,
        scratch=[pltpu.VMEM((BLOCK, GROUP * BLOCK), bf16)] * 2
        + [pltpu.VMEM(values.shape, bf16)] * 2
        + [pltpu.SemaphoreType.DMA((KV_HEADS + 2,))],
        flops=10 * macs,
        exps=HEADS * BLOCK * BLOCK,
    )
    returned = lax.ppermute(halo, ("span", "head"), back)
    own = call(
        own_kernel,
        array((features, BLOCK), f32),
        (weights, dscores, held_queries, held_grads),
        [VMEM] * 4,
        flops=4 * macs,
    )
    send = call(
        sum_kernel,
        array((owners, OWNED + EXTRA, BLOCK), bf16),
        (own, returned, totals),
        [VMEM] * 3,
    )
    got = lax.all_to_all(send, "head", 0, 0, tiled=True)
    return call(
        unpack_kernel,
        (
            array((OWNED, owners * BLOCK), bf16),
            array((HEADS_OWNED, owners * BLOCK), f32),
        ),
        (got,),
        [VMEM],
    )


def solution(mesh):
    return jax.shard_map(
        shards,
        mesh=mesh,
        in_specs=(
            P(("rep", "span", "head"), None),
            P(("rep", "span", "head"), None),
            P(("rep", "span", "head"), None),
            P(("rep", "span"), "head"),
            P("rep"),
        ),
        out_specs=(P("head", ("rep", "span")), P("head", ("rep", "span"))),
        check_vma=False,
    )
```

```python
import math

import jax
import jax.numpy as jnp
from jax import lax
from jax.experimental import pallas as pl
from jax.experimental.pallas import tpu as pltpu
from jax.sharding import PartitionSpec as P

HEADS = 32
KV_HEADS = 4
GROUP = HEADS // KV_HEADS
HEAD_DIM = 128
BLOCK = 128
WIDTH = 2 * BLOCK
DOCS = 32
OWNERS = 16
OWNED = 2 * KV_HEADS * HEAD_DIM // OWNERS
HEADS_OWNED = HEADS // OWNERS
EXTRA = 8
SCALE = 1.0 / math.sqrt(HEAD_DIM)
SCORE_SCALE = SCALE * math.log2(math.e)
NEG = -1e30
PAIRS = GROUP // 2
VMEM = pl.BlockSpec(memory_space=pltpu.VMEM)
SMEM = pl.BlockSpec(memory_space=pltpu.SMEM)
NT = (((1,), (1,)), ((), ()))


def dot(a, b, dims=(((1,), (0,)), ((), ()))):
    return lax.dot_general(a, b, dims, preferred_element_type=jnp.float32)


def pair_rows(ref, pair):
    left = 2 * pair * HEAD_DIM
    return jnp.concatenate(
        [ref[:, left : left + HEAD_DIM], ref[:, left + HEAD_DIM : left + 2 * HEAD_DIM]], 0
    )


def pair_cols(pair):
    return slice(2 * pair * BLOCK, 2 * (pair + 1) * BLOCK)


def twice(x):
    return jnp.concatenate([x, x], 1)


def feature_rows(group, which):
    first = (2 * group + which) * HEAD_DIM
    return slice(first, first + HEAD_DIM)


def head_cols(h):
    return slice(h * HEAD_DIM, (h + 1) * HEAD_DIM)


def forward_kernel(
    base_ref, doc_ref, q_ref, k_ref, v_ref, prev_ref, p_ref, p_prev_ref, total_ref, q_out_ref, v_out_ref
):
    features = KV_HEADS * HEAD_DIM
    q_out_ref[...] = q_ref[...]
    v_out_ref[:BLOCK, :] = prev_ref[:, features:]
    v_out_ref[BLOCK:, :] = v_ref[...]
    base = base_ref[0]
    query_pos = base + lax.broadcasted_iota(jnp.int32, (1, BLOCK), 1)
    doc_first = jnp.zeros((1, BLOCK), jnp.int32)
    start = jnp.int32(0)
    for d in range(DOCS):
        doc_first = jnp.where(start <= query_pos, start, doc_first)
        start = start + doc_ref[d]
    key_pos = base - BLOCK + lax.broadcasted_iota(jnp.int32, (WIDTH, BLOCK), 0)
    bias = twice(jnp.where((key_pos >= doc_first) & (key_pos <= query_pos), 0.0, NEG))
    for g in range(KV_HEADS):
        keys = jnp.concatenate([prev_ref[:, head_cols(g)], k_ref[:, head_cols(g)]], 0)
        for i in range(PAIRS):
            pair = g * PAIRS + i
            s = dot(keys, pair_rows(q_ref, pair), NT) * SCORE_SCALE + bias
            row_max = jnp.max(s, axis=0, keepdims=True)
            e = jnp.exp2(s - row_max)
            total = jnp.sum(e, axis=0, keepdims=True)
            total_ref[pair : pair + 1, :] = (row_max + jnp.log2(total)) * math.log(2.0)
            p = (e * (1.0 / total)).astype(jnp.bfloat16)
            p_prev_ref[g, :, pair_cols(i)] = p[:BLOCK]
            p_ref[g, :, pair_cols(i)] = p[BLOCK:]


def halo_kernel(
    p_ref, p_prev_ref, q_ref, v_ref, og_far_ref, halo_ref, ds_ref, og_ref, ds_prev_ref, sems
):
    og_copies = [
        pltpu.make_async_copy(
            og_far_ref.at[pl.ds(g * PAIRS, PAIRS)], og_ref.at[pl.ds(g * PAIRS, PAIRS)], sems.at[g]
        )
        for g in range(KV_HEADS)
    ]
    for copy in og_copies:
        copy.start()
    for copy in og_copies:
        copy.wait()
    for g in range(KV_HEADS):
        vals = v_ref[:, head_cols(g)]
        queries, grads = [], []
        for i in range(PAIRS):
            pair = g * PAIRS + i
            og = pair_rows(og_ref.at[pair], 0)
            queries.append(pair_rows(q_ref, pair))
            grads.append(og)
            p_prev = p_prev_ref[g, :, pair_cols(i)].astype(jnp.float32)
            p_own = p_ref[g, :, pair_cols(i)].astype(jnp.float32)
            dp = dot(vals, og, NT)
            dp_prev, dp_own = dp[:BLOCK], dp[BLOCK:]
            delta = jnp.sum(p_prev * dp_prev + p_own * dp_own, axis=0, keepdims=True)
            ds_prev_ref[:, pair_cols(i)] = (p_prev * (dp_prev - delta)).astype(jnp.bfloat16)
            ds_ref[g, :, pair_cols(i)] = (p_own * (dp_own - delta)).astype(jnp.bfloat16)
        dk = dot(ds_prev_ref[...], jnp.concatenate(queries, 0)) * SCALE
        dv = dot(p_prev_ref[g], jnp.concatenate(grads, 0))
        halo_ref[feature_rows(g, 0), :] = dk.astype(jnp.bfloat16).T
        halo_ref[feature_rows(g, 1), :] = dv.astype(jnp.bfloat16).T


def own_kernel(p_ref, ds_ref, q_ref, og_ref, own_ref):
    for g in range(KV_HEADS):
        pairs = range(g * PAIRS, (g + 1) * PAIRS)
        queries = jnp.concatenate([pair_rows(q_ref, pair) for pair in pairs], 0)
        grads = jnp.concatenate([pair_rows(og_ref.at[pair], 0) for pair in pairs], 0)
        own_ref[feature_rows(g, 0), :] = (dot(ds_ref[g], queries) * SCALE).T
        own_ref[feature_rows(g, 1), :] = dot(p_ref[g], grads).T


def sum_kernel(own_ref, halo_ref, total_ref, send_ref):
    for z in range(OWNERS):
        rows = slice(z * OWNED, (z + 1) * OWNED)
        send_ref[z, :OWNED, :] = (
            own_ref[rows, :] + halo_ref[rows, :].astype(jnp.float32)
        ).astype(jnp.bfloat16)
        total = total_ref[z : z + 1, :]
        total = jnp.concatenate([total[:, :BLOCK], total[:, BLOCK:]], 0)
        high = total.astype(jnp.bfloat16).astype(jnp.float32)
        low = total - high
        pad = jnp.zeros((EXTRA - 2 * HEADS_OWNED, BLOCK), jnp.float32)
        send_ref[z, OWNED:, :] = jnp.concatenate([high, low, pad], 0).astype(jnp.bfloat16)


def unpack_kernel(got_ref, grads_ref, total_ref):
    for b in range(OWNERS):
        cols = slice(b * BLOCK, (b + 1) * BLOCK)
        grads_ref[:, cols] = got_ref[b, :OWNED, :]
        extra = got_ref[b, OWNED:, :].astype(jnp.float32)
        total_ref[:, cols] = extra[:HEADS_OWNED] + extra[HEADS_OWNED : 2 * HEADS_OWNED]


def call(kernel, out_shape, args, specs, scratch=(), flops=0, exps=0, limit=8):
    outs = jax.tree.leaves(out_shape)
    moved = sum(math.prod(a.shape) * a.dtype.itemsize for a in [*args, *outs])
    return pl.pallas_call(
        kernel,
        out_shape=out_shape,
        in_specs=specs,
        out_specs=jax.tree.map(lambda _: VMEM, out_shape),
        scratch_shapes=scratch,
        compiler_params=pltpu.CompilerParams(vmem_limit_bytes=limit * 2**20),
        cost_estimate=pl.CostEstimate(
            flops=flops, bytes_accessed=moved, transcendentals=exps
        ),
    )(*args)


def shards(queries, keys, values, out_grad, doc_lengths):
    spans, owners = lax.axis_size("span"), lax.axis_size("head")
    block_index = lax.axis_index("span") * owners + lax.axis_index("head")
    blocks = spans * owners
    base = jnp.full((1,), block_index * BLOCK, jnp.int32)
    f32, bf16 = jnp.float32, jnp.bfloat16
    onward = [(i, i + 1) for i in range(blocks - 1)]
    back = [(i + 1, i) for i in range(blocks - 1)]
    og = lax.all_to_all(
        out_grad.reshape(owners, BLOCK, HEADS_OWNED * HEAD_DIM), "head", 0, 0, tiled=True
    )
    prev = lax.ppermute(jnp.concatenate([keys, values], 1), ("span", "head"), onward)
    macs = HEADS * BLOCK * BLOCK * HEAD_DIM
    array = jax.ShapeDtypeStruct
    kept = array((KV_HEADS, BLOCK, GROUP * BLOCK), bf16)
    weights, halo_weights, totals, held_queries, held_values = call(
        forward_kernel,
        (
            kept,
            kept,
            array((owners, HEADS_OWNED * BLOCK), f32),
            array(queries.shape, bf16),
            array((WIDTH, KV_HEADS * HEAD_DIM), bf16),
        ),
        (base, doc_lengths, queries, keys, values, prev),
        [SMEM, SMEM] + [VMEM] * 4,
        flops=20000 * macs,
        exps=HEADS * BLOCK * WIDTH,
    )
    features = 2 * KV_HEADS * HEAD_DIM
    halo, dscores, held_grads = call(
        halo_kernel,
        (array((features, BLOCK), bf16), kept, array(og.shape, bf16)),
        (weights, halo_weights, held_queries, held_values, og),
        [VMEM] * 4 + [pl.BlockSpec(memory_space=pl.ANY)],
        scratch=[
            pltpu.VMEM((BLOCK, GROUP * BLOCK), bf16),
            pltpu.SemaphoreType.DMA((KV_HEADS,)),
        ],
        flops=8 * macs,
    )
    returned = lax.ppermute(halo, ("span", "head"), back)
    own = call(
        own_kernel,
        array((features, BLOCK), f32),
        (weights, dscores, held_queries, held_grads),
        [VMEM] * 4,
        flops=4 * macs,
    )
    send = call(
        sum_kernel,
        array((owners, OWNED + EXTRA, BLOCK), bf16),
        (own, returned, totals),
        [VMEM] * 3,
    )
    got = lax.all_to_all(send, "head", 0, 0, tiled=True)
    return call(
        unpack_kernel,
        (
            array((OWNED, owners * BLOCK), bf16),
            array((HEADS_OWNED, owners * BLOCK), f32),
        ),
        (got,),
        [VMEM],
    )


def solution(mesh):
    return jax.shard_map(
        shards,
        mesh=mesh,
        in_specs=(
            P(("rep", "span", "head"), None),
            P(("rep", "span", "head"), None),
            P(("rep", "span", "head"), None),
            P(("rep", "span"), "head"),
            P("rep"),
        ),
        out_specs=(P("head", ("rep", "span")), P("head", ("rep", "span"))),
        check_vma=False,
    )
```

```python
import math

import jax
import jax.numpy as jnp
from jax import lax
from jax.experimental import pallas as pl
from jax.experimental.pallas import tpu as pltpu
from jax.sharding import PartitionSpec as P

HEADS = 32
KV_HEADS = 4
GROUP = HEADS // KV_HEADS
HEAD_DIM = 128
BLOCK = 128
WIDTH = 2 * BLOCK
DOCS = 32
OWNERS = 16
OWNED = 2 * KV_HEADS * HEAD_DIM // OWNERS
HEADS_OWNED = HEADS // OWNERS
EXTRA = 8
SCALE = 1.0 / math.sqrt(HEAD_DIM)
SCORE_SCALE = SCALE * math.log2(math.e)
NEG = -1e30
PAIRS = GROUP // 2
VMEM = pl.BlockSpec(memory_space=pltpu.VMEM)
SMEM = pl.BlockSpec(memory_space=pltpu.SMEM)
NT = (((1,), (1,)), ((), ()))


def dot(a, b, dims=(((1,), (0,)), ((), ()))):
    return lax.dot_general(a, b, dims, preferred_element_type=jnp.float32)


def feature_rows(group, which):
    first = (2 * group + which) * HEAD_DIM
    return slice(first, first + HEAD_DIM)


def head_cols(h):
    return slice(h * HEAD_DIM, (h + 1) * HEAD_DIM)


def forward_kernel(
    base_ref, doc_ref, q_ref, k_ref, v_ref, prev_ref, p_ref, total_ref, qt_ref, v_out_ref
):
    features = KV_HEADS * HEAD_DIM
    v_out_ref[:BLOCK, :] = prev_ref[:, features:]
    v_out_ref[BLOCK:, :] = v_ref[...]
    base = base_ref[0]
    query_pos = base + lax.broadcasted_iota(jnp.int32, (BLOCK, 1), 0)
    doc_first = jnp.zeros((BLOCK, 1), jnp.int32)
    start = jnp.int32(0)
    for d in range(DOCS):
        doc_first = jnp.where(start <= query_pos, start, doc_first)
        start = start + doc_ref[d]
    key_pos = base - BLOCK + lax.broadcasted_iota(jnp.int32, (BLOCK, WIDTH), 1)
    bias = jnp.where((key_pos >= doc_first) & (key_pos <= query_pos), 0.0, NEG)
    for g in range(KV_HEADS):
        keys = jnp.concatenate([prev_ref[:, head_cols(g)], k_ref[:, head_cols(g)]], 0)
        for h in range(GROUP):
            head = g * GROUP + h
            q = q_ref[:, head_cols(head)]
            qt_ref[g, :, head_cols(h)] = q.T
            s = dot(q, keys, NT) * SCORE_SCALE + bias
            row_max = jnp.max(s, axis=1, keepdims=True)
            e = jnp.exp2(s - row_max)
            total = jnp.sum(e, axis=1, keepdims=True)
            log_total = (row_max + jnp.log2(total)) * math.log(2.0)
            total_ref[head : head + 1, :] = jnp.broadcast_to(log_total, (BLOCK, BLOCK)).T[:1]
            p_ref[g, head_cols(h), :] = (e * (1.0 / total)).astype(jnp.bfloat16)


def backward_kernel(p_ref, qt_ref, v_ref, og_far_ref, halo_ref, own_ref, og_ref, sems):
    copies = [
        pltpu.make_async_copy(
            og_far_ref.at[pl.ds(g * PAIRS, PAIRS)], og_ref.at[pl.ds(g * PAIRS, PAIRS)], sems.at[g]
        )
        for g in range(KV_HEADS)
    ]
    for copy in copies:
        copy.start()
    for copy in copies:
        copy.wait()
    for g in range(KV_HEADS):
        vals = v_ref[:, head_cols(g)]
        dss, ogs = [], []
        for h in range(GROUP):
            og = og_ref[g * PAIRS + h // 2, :, head_cols(h % 2)]
            dp = dot(og, vals, NT)
            p = p_ref[g, h * BLOCK : (h + 1) * BLOCK, :].astype(jnp.float32)
            delta = jnp.sum(p * dp, axis=1, keepdims=True)
            dss.append((p * (dp - delta)).astype(jnp.bfloat16))
            ogs.append(og.T)
        dk = dot(qt_ref[g], jnp.concatenate(dss, 0)) * SCALE
        dv = dot(jnp.concatenate(ogs, 1), p_ref[g])
        for i, grad in enumerate((dk, dv)):
            halo_ref[feature_rows(g, i), :] = grad[:, :BLOCK].astype(jnp.bfloat16)
            own_ref[feature_rows(g, i), :] = grad[:, BLOCK:]


def sum_kernel(own_ref, halo_ref, total_ref, send_ref):
    for z in range(OWNERS):
        rows = slice(z * OWNED, (z + 1) * OWNED)
        send_ref[z, :OWNED, :] = (
            own_ref[rows, :] + halo_ref[rows, :].astype(jnp.float32)
        ).astype(jnp.bfloat16)
        total = total_ref[z * HEADS_OWNED : (z + 1) * HEADS_OWNED, :]
        high = total.astype(jnp.bfloat16).astype(jnp.float32)
        low = total - high
        pad = jnp.zeros((EXTRA - 2 * HEADS_OWNED, BLOCK), jnp.float32)
        send_ref[z, OWNED:, :] = jnp.concatenate([high, low, pad], 0).astype(jnp.bfloat16)


def unpack_kernel(got_ref, grads_ref, total_ref):
    for b in range(OWNERS):
        cols = slice(b * BLOCK, (b + 1) * BLOCK)
        grads_ref[:, cols] = got_ref[b, :OWNED, :]
        extra = got_ref[b, OWNED:, :].astype(jnp.float32)
        total_ref[:, cols] = extra[:HEADS_OWNED] + extra[HEADS_OWNED : 2 * HEADS_OWNED]


def call(kernel, out_shape, args, specs, scratch=(), flops=0, exps=0, limit=8):
    outs = jax.tree.leaves(out_shape)
    moved = sum(math.prod(a.shape) * a.dtype.itemsize for a in [*args, *outs])
    return pl.pallas_call(
        kernel,
        out_shape=out_shape,
        in_specs=specs,
        out_specs=jax.tree.map(lambda _: VMEM, out_shape),
        scratch_shapes=scratch,
        compiler_params=pltpu.CompilerParams(vmem_limit_bytes=limit * 2**20),
        cost_estimate=pl.CostEstimate(
            flops=flops, bytes_accessed=moved, transcendentals=exps
        ),
    )(*args)


def shards(queries, keys, values, out_grad, doc_lengths):
    spans, owners = lax.axis_size("span"), lax.axis_size("head")
    block_index = lax.axis_index("span") * owners + lax.axis_index("head")
    blocks = spans * owners
    base = jnp.full((1,), block_index * BLOCK, jnp.int32)
    f32, bf16 = jnp.float32, jnp.bfloat16
    onward = [(i, i + 1) for i in range(blocks - 1)]
    back = [(i + 1, i) for i in range(blocks - 1)]
    og = lax.all_to_all(
        out_grad.reshape(owners, BLOCK, HEADS_OWNED * HEAD_DIM), "head", 0, 0, tiled=True
    )
    prev = lax.ppermute(jnp.concatenate([keys, values], 1), ("span", "head"), onward)
    macs = HEADS * BLOCK * BLOCK * HEAD_DIM
    array = jax.ShapeDtypeStruct
    weights, totals, turned_queries, held_values = call(
        forward_kernel,
        (
            array((KV_HEADS, GROUP * BLOCK, WIDTH), bf16),
            array((HEADS, BLOCK), f32),
            array((KV_HEADS, HEAD_DIM, GROUP * BLOCK), bf16),
            array((WIDTH, KV_HEADS * HEAD_DIM), bf16),
        ),
        (base, doc_lengths, queries, keys, values, prev),
        [SMEM, SMEM] + [VMEM] * 4,
        flops=20000 * macs,
        exps=HEADS * BLOCK * WIDTH,
    )
    features = 2 * KV_HEADS * HEAD_DIM
    halo, own = call(
        backward_kernel,
        (array((features, BLOCK), bf16), array((features, BLOCK), f32)),
        (weights, turned_queries, held_values, og),
        [VMEM] * 3 + [pl.BlockSpec(memory_space=pl.ANY)],
        scratch=[
            pltpu.VMEM((owners, BLOCK, HEADS_OWNED * HEAD_DIM), bf16),
            pltpu.SemaphoreType.DMA((KV_HEADS,)),
        ],
        flops=12 * macs,
    )
    returned = lax.ppermute(halo, ("span", "head"), back)
    send = call(
        sum_kernel,
        array((owners, OWNED + EXTRA, BLOCK), bf16),
        (own, returned, totals),
        [VMEM] * 3,
    )
    got = lax.all_to_all(send, "head", 0, 0, tiled=True)
    return call(
        unpack_kernel,
        (
            array((OWNED, owners * BLOCK), bf16),
            array((HEADS_OWNED, owners * BLOCK), f32),
        ),
        (got,),
        [VMEM],
    )


def solution(mesh):
    return jax.shard_map(
        shards,
        mesh=mesh,
        in_specs=(
            P(("rep", "span", "head"), None),
            P(("rep", "span", "head"), None),
            P(("rep", "span", "head"), None),
            P(("rep", "span"), "head"),
            P("rep"),
        ),
        out_specs=(P("head", ("rep", "span")), P("head", ("rep", "span"))),
        check_vma=False,
    )
```

```python
import math

import jax
import jax.numpy as jnp
from jax import lax
from jax.experimental import pallas as pl
from jax.experimental.pallas import tpu as pltpu
from jax.sharding import PartitionSpec as P

HEADS = 32
KV_HEADS = 4
GROUP = HEADS // KV_HEADS
HEAD_DIM = 128
BLOCK = 128
WIDTH = 2 * BLOCK
DOCS = 32
OWNERS = 16
OWNED = 2 * KV_HEADS * HEAD_DIM // OWNERS
HEADS_OWNED = HEADS // OWNERS
EXTRA = 8
SCALE = 1.0 / math.sqrt(HEAD_DIM)
SCORE_SCALE = SCALE * math.log2(math.e)
NEG = -1e30
PAIRS = GROUP // 2
VMEM = pl.BlockSpec(memory_space=pltpu.VMEM)
SMEM = pl.BlockSpec(memory_space=pltpu.SMEM)
NT = (((1,), (1,)), ((), ()))


def dot(a, b, dims=(((1,), (0,)), ((), ()))):
    return lax.dot_general(a, b, dims, preferred_element_type=jnp.float32)


def feature_rows(group, which):
    first = (2 * group + which) * HEAD_DIM
    return slice(first, first + HEAD_DIM)


def head_cols(h):
    return slice(h * HEAD_DIM, (h + 1) * HEAD_DIM)


def forward_kernel(
    base_ref, doc_ref, q_ref, k_ref, k_prev_ref, p_ref, total_ref, qt_ref
):
    base = base_ref[0]
    query_pos = base + lax.broadcasted_iota(jnp.int32, (BLOCK, 1), 0)
    doc_first = jnp.zeros((BLOCK, 1), jnp.int32)
    start = jnp.int32(0)
    for d in range(DOCS):
        doc_first = jnp.where(start <= query_pos, start, doc_first)
        start = start + doc_ref[d]
    key_pos = base - BLOCK + lax.broadcasted_iota(jnp.int32, (BLOCK, WIDTH), 1)
    bias = jnp.where((key_pos >= doc_first) & (key_pos <= query_pos), 0.0, NEG)
    for g in range(KV_HEADS):
        keys = jnp.concatenate([k_prev_ref[:, head_cols(g)], k_ref[:, head_cols(g)]], 0)
        for h in range(GROUP):
            head = g * GROUP + h
            q = q_ref[:, head_cols(head)]
            qt_ref[g, :, head_cols(h)] = q.T
            s = dot(q, keys, NT) * SCORE_SCALE + bias
            row_max = jnp.max(s, axis=1, keepdims=True)
            e = jnp.exp2(s - row_max)
            total = jnp.sum(e, axis=1, keepdims=True)
            log_total = (row_max + jnp.log2(total)) * math.log(2.0)
            total_ref[head : head + 1, :] = jnp.broadcast_to(log_total, (BLOCK, BLOCK)).T[:1]
            p_ref[g, head_cols(h), :] = (e * (1.0 / total)).astype(jnp.bfloat16)


def value_grads_kernel(p_ref, og_far_ref, dv_ref, og_ref, sems):
    copies = [
        pltpu.make_async_copy(
            og_far_ref.at[pl.ds(g * PAIRS, PAIRS)], og_ref.at[pl.ds(g * PAIRS, PAIRS)], sems.at[g]
        )
        for g in range(KV_HEADS)
    ]
    for copy in copies:
        copy.start()
    for copy in copies:
        copy.wait()
    for g in range(KV_HEADS):
        turned = [og_ref[g * PAIRS + h // 2, :, head_cols(h % 2)].T for h in range(GROUP)]
        dv_ref[head_cols(g), :] = dot(jnp.concatenate(turned, 1), p_ref[g])


def key_grads_kernel(p_ref, qt_ref, v_ref, v_prev_ref, og_ref, dv_ref, halo_ref, own_ref):
    for g in range(KV_HEADS):
        vals = jnp.concatenate([v_prev_ref[:, head_cols(g)], v_ref[:, head_cols(g)]], 0)
        dscores = []
        for h in range(GROUP):
            og = og_ref[g * PAIRS + h // 2, :, head_cols(h % 2)]
            dp = dot(og, vals, NT)
            p = p_ref[g, head_cols(h), :].astype(jnp.float32)
            delta = jnp.sum(p * dp, axis=1, keepdims=True)
            dscores.append((p * (dp - delta)).astype(jnp.bfloat16))
        dk = dot(qt_ref[g], jnp.concatenate(dscores, 0)) * SCALE
        for i, grad in enumerate((dk, dv_ref[head_cols(g), :])):
            halo_ref[feature_rows(g, i), :] = grad[:, :BLOCK].astype(jnp.bfloat16)
            own_ref[feature_rows(g, i), :] = grad[:, BLOCK:]


def sum_kernel(own_ref, halo_ref, total_ref, send_ref):
    for z in range(OWNERS):
        rows = slice(z * OWNED, (z + 1) * OWNED)
        send_ref[z, :OWNED, :] = (
            own_ref[rows, :] + halo_ref[rows, :].astype(jnp.float32)
        ).astype(jnp.bfloat16)
        total = total_ref[z * HEADS_OWNED : (z + 1) * HEADS_OWNED, :]
        high = total.astype(jnp.bfloat16).astype(jnp.float32)
        low = total - high
        pad = jnp.zeros((EXTRA - 2 * HEADS_OWNED, BLOCK), jnp.float32)
        send_ref[z, OWNED:, :] = jnp.concatenate([high, low, pad], 0).astype(jnp.bfloat16)


def unpack_kernel(got_ref, grads_ref, total_ref):
    for b in range(OWNERS):
        cols = slice(b * BLOCK, (b + 1) * BLOCK)
        grads_ref[:, cols] = got_ref[b, :OWNED, :]
        extra = got_ref[b, OWNED:, :].astype(jnp.float32)
        total_ref[:, cols] = extra[:HEADS_OWNED] + extra[HEADS_OWNED : 2 * HEADS_OWNED]


def call(kernel, out_shape, args, specs, scratch=(), flops=0, exps=0, limit=8):
    outs = jax.tree.leaves(out_shape)
    moved = sum(math.prod(a.shape) * a.dtype.itemsize for a in [*args, *outs])
    return pl.pallas_call(
        kernel,
        out_shape=out_shape,
        in_specs=specs,
        out_specs=jax.tree.map(lambda _: VMEM, out_shape),
        scratch_shapes=scratch,
        compiler_params=pltpu.CompilerParams(vmem_limit_bytes=limit * 2**20),
        cost_estimate=pl.CostEstimate(
            flops=flops, bytes_accessed=moved, transcendentals=exps
        ),
    )(*args)


def shards(queries, keys, values, out_grad, doc_lengths):
    spans, owners = lax.axis_size("span"), lax.axis_size("head")
    block_index = lax.axis_index("span") * owners + lax.axis_index("head")
    blocks = spans * owners
    base = jnp.full((1,), block_index * BLOCK, jnp.int32)
    f32, bf16 = jnp.float32, jnp.bfloat16
    onward = [(i, i + 1) for i in range(blocks - 1)]
    back = [(i + 1, i) for i in range(blocks - 1)]
    og = lax.all_to_all(
        out_grad.reshape(owners, BLOCK, HEADS_OWNED * HEAD_DIM), "head", 0, 0, tiled=True
    )
    k_prev = lax.ppermute(keys, ("span", "head"), onward)
    v_prev = lax.ppermute(values, ("span", "head"), onward)
    macs = HEADS * BLOCK * BLOCK * HEAD_DIM
    array = jax.ShapeDtypeStruct
    weights, totals, turned_queries = call(
        forward_kernel,
        (
            array((KV_HEADS, GROUP * BLOCK, WIDTH), bf16),
            array((HEADS, BLOCK), f32),
            array((KV_HEADS, HEAD_DIM, GROUP * BLOCK), bf16),
        ),
        (base, doc_lengths, queries, keys, k_prev),
        [SMEM, SMEM] + [VMEM] * 3,
        flops=20000 * macs,
        exps=HEADS * BLOCK * WIDTH,
    )
    features = 2 * KV_HEADS * HEAD_DIM
    any_space = pl.BlockSpec(memory_space=pl.ANY)
    value_grads, held_grads = call(
        value_grads_kernel,
        (array((KV_HEADS * HEAD_DIM, WIDTH), f32), array(og.shape, bf16)),
        (weights, og),
        [VMEM, any_space],
        scratch=[pltpu.SemaphoreType.DMA((KV_HEADS,))],
        flops=4 * macs,
    )
    halo, own = call(
        key_grads_kernel,
        (array((features, BLOCK), bf16), array((features, BLOCK), f32)),
        (weights, turned_queries, values, v_prev, held_grads, value_grads),
        [VMEM] * 6,
        flops=8 * macs,
    )
    returned = lax.ppermute(halo, ("span", "head"), back)
    send = call(
        sum_kernel,
        array((owners, OWNED + EXTRA, BLOCK), bf16),
        (own, returned, totals),
        [VMEM] * 3,
    )
    got = lax.all_to_all(send, "head", 0, 0, tiled=True)
    return call(
        unpack_kernel,
        (
            array((OWNED, owners * BLOCK), bf16),
            array((HEADS_OWNED, owners * BLOCK), f32),
        ),
        (got,),
        [VMEM],
    )


def solution(mesh):
    return jax.shard_map(
        shards,
        mesh=mesh,
        in_specs=(
            P(("rep", "span", "head"), None),
            P(("rep", "span", "head"), None),
            P(("rep", "span", "head"), None),
            P(("rep", "span"), "head"),
            P("rep"),
        ),
        out_specs=(P("head", ("rep", "span")), P("head", ("rep", "span"))),
        check_vma=False,
    )
```

```python
import math

import jax
import jax.numpy as jnp
from jax import lax
from jax.experimental import pallas as pl
from jax.experimental.pallas import tpu as pltpu
from jax.sharding import PartitionSpec as P

HEADS = 32
KV_HEADS = 4
GROUP = HEADS // KV_HEADS
HEAD_DIM = 128
BLOCK = 128
WIDTH = 2 * BLOCK
DOCS = 32
OWNERS = 16
OWNED = 2 * KV_HEADS * HEAD_DIM // OWNERS
HEADS_OWNED = HEADS // OWNERS
EXTRA = 8
SCALE = 1.0 / math.sqrt(HEAD_DIM)
SCORE_SCALE = SCALE * math.log2(math.e)
NEG = -1e30
PAIRS = GROUP // 2
VMEM = pl.BlockSpec(memory_space=pltpu.VMEM)
SMEM = pl.BlockSpec(memory_space=pltpu.SMEM)
NT = (((1,), (1,)), ((), ()))


def dot(a, b, dims=(((1,), (0,)), ((), ()))):
    return lax.dot_general(a, b, dims, preferred_element_type=jnp.float32)


def feature_rows(group, which):
    first = (2 * group + which) * HEAD_DIM
    return slice(first, first + HEAD_DIM)


def head_cols(h):
    return slice(h * HEAD_DIM, (h + 1) * HEAD_DIM)


def forward_kernel(
    base_ref, doc_ref, q_ref, k_ref, v_ref, prev_ref, p_ref, total_ref, qt_ref, v_out_ref
):
    v_out_ref[:BLOCK, :] = prev_ref[BLOCK:, :]
    v_out_ref[BLOCK:, :] = v_ref[...]
    base = base_ref[0]
    query_pos = base + lax.broadcasted_iota(jnp.int32, (BLOCK, 1), 0)
    doc_first = jnp.zeros((BLOCK, 1), jnp.int32)
    start = jnp.int32(0)
    for d in range(DOCS):
        doc_first = jnp.where(start <= query_pos, start, doc_first)
        start = start + doc_ref[d]
    key_pos = base - BLOCK + lax.broadcasted_iota(jnp.int32, (BLOCK, WIDTH), 1)
    bias = jnp.where((key_pos >= doc_first) & (key_pos <= query_pos), 0.0, NEG)
    for g in range(KV_HEADS):
        keys = jnp.concatenate([prev_ref[:BLOCK, head_cols(g)], k_ref[:, head_cols(g)]], 0)
        for h in range(GROUP):
            head = g * GROUP + h
            q = q_ref[:, head_cols(head)]
            qt_ref[g, :, head_cols(h)] = q.T
            s = dot(q, keys, NT) * SCORE_SCALE + bias
            row_max = jnp.max(s, axis=1, keepdims=True)
            e = jnp.exp2(s - row_max)
            total = jnp.sum(e, axis=1, keepdims=True)
            log_total = (row_max + jnp.log2(total)) * math.log(2.0)
            total_ref[head : head + 1, :] = jnp.broadcast_to(log_total, (BLOCK, BLOCK)).T[:1]
            p_ref[g, head_cols(h), :] = (e * (1.0 / total)).astype(jnp.bfloat16)


def backward_kernel(p_ref, qt_ref, v_ref, og_far_ref, halo_ref, own_ref, og_ref, sems):
    copies = [
        pltpu.make_async_copy(
            og_far_ref.at[pl.ds(g * PAIRS, PAIRS)], og_ref.at[pl.ds(g * PAIRS, PAIRS)], sems.at[g]
        )
        for g in range(KV_HEADS)
    ]
    for copy in copies:
        copy.start()
    for copy in copies:
        copy.wait()
    for g in range(KV_HEADS):
        vals = v_ref[:, head_cols(g)]
        dss, ogs = [], []
        for h in range(GROUP):
            og = og_ref[g * PAIRS + h // 2, :, head_cols(h % 2)]
            dp = dot(og, vals, NT)
            p = p_ref[g, h * BLOCK : (h + 1) * BLOCK, :].astype(jnp.float32)
            delta = jnp.sum(p * dp, axis=1, keepdims=True)
            dss.append((p * (dp - delta)).astype(jnp.bfloat16))
            ogs.append(og.T)
        dk = dot(qt_ref[g], jnp.concatenate(dss, 0)) * SCALE
        dv = dot(jnp.concatenate(ogs, 1), p_ref[g])
        for i, grad in enumerate((dk, dv)):
            halo_ref[feature_rows(g, i), :] = grad[:, :BLOCK].astype(jnp.bfloat16)
            own_ref[feature_rows(g, i), :] = grad[:, BLOCK:]


def sum_kernel(own_ref, halo_ref, total_ref, send_ref):
    for z in range(OWNERS):
        rows = slice(z * OWNED, (z + 1) * OWNED)
        send_ref[z, :OWNED, :] = (
            own_ref[rows, :] + halo_ref[rows, :].astype(jnp.float32)
        ).astype(jnp.bfloat16)
        total = total_ref[z * HEADS_OWNED : (z + 1) * HEADS_OWNED, :]
        high = total.astype(jnp.bfloat16).astype(jnp.float32)
        low = total - high
        pad = jnp.zeros((EXTRA - 2 * HEADS_OWNED, BLOCK), jnp.float32)
        send_ref[z, OWNED:, :] = jnp.concatenate([high, low, pad], 0).astype(jnp.bfloat16)


def unpack_kernel(got_ref, grads_ref, total_ref, sems):
    copies = [
        pltpu.make_async_copy(
            got_ref.at[b, pl.ds(0, OWNED)], grads_ref.at[:, pl.ds(b * BLOCK, BLOCK)], sems.at[b]
        )
        for b in range(OWNERS)
    ]
    for copy in copies:
        copy.start()
    for b in range(OWNERS):
        extra = got_ref[b, OWNED:, :].astype(jnp.float32)
        total_ref[:, b * BLOCK : (b + 1) * BLOCK] = (
            extra[:HEADS_OWNED] + extra[HEADS_OWNED : 2 * HEADS_OWNED]
        )
    for copy in copies:
        copy.wait()


def call(kernel, out_shape, args, specs, scratch=(), out_specs=None, flops=0, exps=0, limit=8):
    outs = jax.tree.leaves(out_shape)
    moved = sum(math.prod(a.shape) * a.dtype.itemsize for a in [*args, *outs])
    return pl.pallas_call(
        kernel,
        out_shape=out_shape,
        in_specs=specs,
        out_specs=out_specs or jax.tree.map(lambda _: VMEM, out_shape),
        scratch_shapes=scratch,
        compiler_params=pltpu.CompilerParams(vmem_limit_bytes=limit * 2**20),
        cost_estimate=pl.CostEstimate(
            flops=flops, bytes_accessed=moved, transcendentals=exps
        ),
    )(*args)


def shards(queries, keys, values, out_grad, doc_lengths):
    spans, owners = lax.axis_size("span"), lax.axis_size("head")
    block_index = lax.axis_index("span") * owners + lax.axis_index("head")
    blocks = spans * owners
    base = jnp.full((1,), block_index * BLOCK, jnp.int32)
    f32, bf16 = jnp.float32, jnp.bfloat16
    onward = [(i, i + 1) for i in range(blocks - 1)]
    back = [(i + 1, i) for i in range(blocks - 1)]
    og = lax.all_to_all(
        out_grad.reshape(owners, BLOCK, HEADS_OWNED * HEAD_DIM), "head", 0, 0, tiled=True
    )
    prev = lax.ppermute(jnp.concatenate([keys, values], 0), ("span", "head"), onward)
    macs = HEADS * BLOCK * BLOCK * HEAD_DIM
    array = jax.ShapeDtypeStruct
    weights, totals, turned_queries, held_values = call(
        forward_kernel,
        (
            array((KV_HEADS, GROUP * BLOCK, WIDTH), bf16),
            array((HEADS, BLOCK), f32),
            array((KV_HEADS, HEAD_DIM, GROUP * BLOCK), bf16),
            array((WIDTH, KV_HEADS * HEAD_DIM), bf16),
        ),
        (base, doc_lengths, queries, keys, values, prev),
        [SMEM, SMEM] + [VMEM] * 4,
        flops=20000 * macs,
        exps=HEADS * BLOCK * WIDTH,
    )
    features = 2 * KV_HEADS * HEAD_DIM
    halo, own = call(
        backward_kernel,
        (array((features, BLOCK), bf16), array((features, BLOCK), f32)),
        (weights, turned_queries, held_values, og),
        [VMEM] * 3 + [pl.BlockSpec(memory_space=pl.ANY)],
        scratch=[
            pltpu.VMEM((owners, BLOCK, HEADS_OWNED * HEAD_DIM), bf16),
            pltpu.SemaphoreType.DMA((KV_HEADS,)),
        ],
        flops=12 * macs,
    )
    returned = lax.ppermute(halo, ("span", "head"), back)
    send = call(
        sum_kernel,
        array((owners, OWNED + EXTRA, BLOCK), bf16),
        (own, returned, totals),
        [VMEM] * 3,
    )
    got = lax.all_to_all(send, "head", 0, 0, tiled=True)
    return call(
        unpack_kernel,
        (
            array((OWNED, owners * BLOCK), bf16),
            array((HEADS_OWNED, owners * BLOCK), f32),
        ),
        (got,),
        [VMEM],
        scratch=[pltpu.SemaphoreType.DMA((OWNERS,))],
        out_specs=(pl.BlockSpec(memory_space=pl.ANY), VMEM),
    )


def solution(mesh):
    return jax.shard_map(
        shards,
        mesh=mesh,
        in_specs=(
            P(("rep", "span", "head"), None),
            P(("rep", "span", "head"), None),
            P(("rep", "span", "head"), None),
            P(("rep", "span"), "head"),
            P("rep"),
        ),
        out_specs=(P("head", ("rep", "span")), P("head", ("rep", "span"))),
        check_vma=False,
    )
```
